32 devices in a mesh: req: 16 (over z, x, core), head: 2 (over y).
Axes of the slice: x: 2, y: 2, z: 4, core: 2. Of those that a mesh axis runs over, the one named last changes fastest.
Arguments:
- queries: bfloat16 [32, 256, 64, 128], P('req', None, 'head'), may hold values from -9 to 9
- fresh_key_value: bfloat16 [2, 32, 256, 8, 128], P(None, 'req', None, 'head'), may hold values from -6 to 6
- prefix_kv: bfloat16 [2, 32, 8, 128, 128], P(None, 'req', 'head'), may hold values from -6 to 6
- block_mask: int32 [32, 32], P('req'), may hold values from 0 to 1, as said below
- valid_tokens: int32 [32], replicated, may hold values from 1 to 128, as said below
Outputs:
- context: bfloat16 [8192, 8192], P(('req', 'head'))
The draws below stay inside these ranges and needn't reach their ends.
Inputs may be any that keep to these rules, and one draw needn't show every extreme that they name: `block_mask`: row r marks the blocks on the path from block 0 down to one block of a prefix tree in which every block's parent has a lower index; a path holds at most 6 blocks, and row 0 holds exactly 6. A path holds at most one block of each aligned group of 2 blocks; block 1 is read by no request. The requests of one index of req read at most 2 blocks of one aligned group, and those of index 0 read exactly 2 blocks of group 1. `valid_tokens`: A block that is the parent of some block holds 128 tokens; block 0 is such a block.
All inputs are finite; a program needn't handle non-finite values.
Results may differ from the reference program's by a relative error of at most 0.006.
Values may be sent and summed in bfloat16 or wider, within the bound.
A program may use at most 128 MiB of HBM per device.

```python
import jax
import jax.numpy as jnp
from jax import lax

QUERY_HEADS = 64
KEY_VALUE_HEADS = 8
HEAD_WIDTH = 128
NEW_TOKENS = 256
BLOCKS_DEV = 2
BLOCK_SLOTS = 128
PATH_BLOCKS = 6
CAP = 2
REQUEST_COUNT = 32
PREFIX_COUNT = 32


def prefix_tree(key):
    base = jax.random.fold_in(key, 11)
    picks = jax.random.randint(jax.random.fold_in(base, 1), (PREFIX_COUNT,), 0, 1 << 30)

    def place(position, carried):
        parents, depths = carried
        group = position // BLOCKS_DEV
        span = jnp.maximum((group - 1) * BLOCKS_DEV + 1, 1)
        drawn = picks[position] % span
        candidate = jnp.where(drawn == 0, 0, BLOCKS_DEV + drawn - 1)
        chained = (position % BLOCKS_DEV == 0) & (group < PATH_BLOCKS)
        candidate = jnp.where(chained, jnp.maximum(position - BLOCKS_DEV, 0), candidate)
        candidate = jnp.where(depths[candidate] >= PATH_BLOCKS, parents[candidate], candidate)
        candidate = jnp.where(group == 0, 0, candidate).astype(jnp.int32)
        parents = parents.at[position].set(candidate)
        depths = depths.at[position].set(jnp.where(group == 0, 1, depths[candidate] + 1))
        return (parents, depths)
    parents = jnp.zeros((PREFIX_COUNT,), jnp.int32)
    depths = jnp.ones((PREFIX_COUNT,), jnp.int32)
    parents, depths = lax.fori_loop(1, PREFIX_COUNT, place, (parents, depths))
    drawn_leaves = jax.random.randint(jax.random.fold_in(base, 2), (REQUEST_COUNT,), 0, PREFIX_COUNT - BLOCKS_DEV + 1)
    leaves = jnp.where(drawn_leaves == 0, 0, BLOCKS_DEV + drawn_leaves - 1).astype(jnp.int32)
    leaves = leaves.at[0].set((PATH_BLOCKS - 1) * BLOCKS_DEV)
    extra = jnp.arange(1, CAP, dtype=jnp.int32)
    leaves = leaves.at[extra].set(BLOCKS_DEV + extra)
    return (parents, leaves)


def draw_block_mask(key, part):
    parents, leaves = prefix_tree(key)
    marks = jnp.zeros((REQUEST_COUNT, PREFIX_COUNT), jnp.int32)
    node_now = leaves
    for level in range(PATH_BLOCKS):
        onehot = (node_now[:, None] == jnp.arange(PREFIX_COUNT)[None, :]).astype(jnp.int32)
        marks = jnp.maximum(marks, onehot)
        node_now = parents[node_now]
    return marks


def draw_valid_tokens(key, part):
    parents, leaves = prefix_tree(key)
    has_child = jnp.zeros((PREFIX_COUNT,), jnp.int32).at[parents[1:]].set(1)
    partial_value = jax.random.randint(jax.random.fold_in(key, 13), (PREFIX_COUNT,), 1, BLOCK_SLOTS + 1)
    return jnp.where(has_child == 1, BLOCK_SLOTS, partial_value).astype(jnp.int32)


def draw_prefix_kv(key, part):
    array_shape = (2, PREFIX_COUNT, KEY_VALUE_HEADS, BLOCK_SLOTS, HEAD_WIDTH)
    return jnp.clip(jax.random.normal(key, array_shape, jnp.float32), -6.0, 6.0).astype(jnp.bfloat16)


def draw_queries(key, part):
    array_shape = (REQUEST_COUNT, NEW_TOKENS, QUERY_HEADS, HEAD_WIDTH)
    return jnp.clip(jax.random.normal(jax.random.fold_in(key, 2), array_shape, jnp.float32), -6.0, 6.0).astype(jnp.bfloat16)


def steps_of(stream_key, dims, shards, least, largest):
    level = 1.0
    for axis_at, parts in shards:
        draws = jax.random.uniform(jax.random.fold_in(jax.random.fold_in(stream_key, 6), axis_at), (parts,), jnp.float32, least / len(shards), largest / len(shards))
        level = level * jnp.repeat(jnp.exp(draws), dims[axis_at] // parts).reshape((-1,) + (1,) * (len(dims) - 1 - axis_at))
    return level


def bell_draw(stream_key, extent, scale, limit, pieces=(), held_as=jnp.bfloat16):
    loudness = steps_of(stream_key, extent, pieces, -0.22, 0.18) if pieces else 1.0
    result = jax.random.normal(stream_key, extent, jnp.float32) * scale * loudness
    return jnp.minimum(jnp.maximum(result, -limit), limit).astype(held_as)


def setup_inputs(seed: int = 0) -> dict:
    splits = jax.random.split(jax.random.key(seed), 6)
    return {
        "queries": draw_queries(jax.random.fold_in(splits[5], 71), 0),
        "fresh_key_value": bell_draw(splits[1], (2, REQUEST_COUNT, NEW_TOKENS, KEY_VALUE_HEADS, HEAD_WIDTH), 1.0, 6.0, ((1, 16), (3, 2))),
        "prefix_kv": draw_prefix_kv(jax.random.fold_in(splits[5], 71), 0),
        "block_mask": draw_block_mask(jax.random.fold_in(splits[5], 71), 0),
        "valid_tokens": draw_valid_tokens(jax.random.fold_in(splits[5], 71), 0),
    }


masked_score = -1e30


def request_context(request_query_rows, request_kv, mask_row, prefix_kv, valid_tokens):
    blocks_all = mask_row.shape[0]
    ranking = mask_row * blocks_all + (blocks_all - 1 - jnp.arange(blocks_all, dtype=jnp.int32))
    _, chosen = lax.top_k(ranking, PATH_BLOCKS)
    chosen = chosen.astype(jnp.int32)
    taken = mask_row[chosen]
    picked_blocks = prefix_kv[:, chosen]
    picked_blocks = jnp.transpose(picked_blocks, (0, 2, 1, 3, 4)).reshape(2, KEY_VALUE_HEADS, PATH_BLOCKS * BLOCK_SLOTS, HEAD_WIDTH)
    own_kv = jnp.transpose(request_kv, (0, 2, 1, 3))
    all_kv = jnp.concatenate([picked_blocks, own_kv], axis=2).astype(jnp.float32)
    prefix_allowed = (taken[:, None] == 1) & (jnp.arange(BLOCK_SLOTS)[None, :] < valid_tokens[chosen][:, None])
    prefix_allowed = jnp.broadcast_to(prefix_allowed.reshape(1, PATH_BLOCKS * BLOCK_SLOTS), (NEW_TOKENS, PATH_BLOCKS * BLOCK_SLOTS))
    causal = jnp.arange(NEW_TOKENS)[:, None] >= jnp.arange(NEW_TOKENS)[None, :]
    allowed = jnp.concatenate([prefix_allowed, causal], axis=1)
    grouped_heads = request_query_rows.reshape(NEW_TOKENS, KEY_VALUE_HEADS, QUERY_HEADS // KEY_VALUE_HEADS, HEAD_WIDTH).astype(jnp.float32)
    scores = jnp.einsum('tkgd,kjd->tkgj', grouped_heads, all_kv[0]) * (HEAD_WIDTH ** -0.5)
    scores = jnp.where(allowed[:, None, None, :], scores, masked_score)
    maxima = jnp.max(scores, axis=-1, keepdims=True)
    weights = jnp.where(allowed[:, None, None, :], jnp.exp(scores - maxima), 0.0)
    totals = jnp.sum(weights, axis=-1, keepdims=True)
    rounded = lax.optimization_barrier(weights.astype(jnp.bfloat16)).astype(jnp.float32)
    context = jnp.einsum('tkgj,kjd->tkgd', rounded, all_kv[1]) / totals
    return context.reshape(NEW_TOKENS, QUERY_HEADS * HEAD_WIDTH).astype(jnp.bfloat16)


def reference(queries, fresh_key_value, prefix_kv, block_mask, valid_tokens):
    def one_request(packed):
        request_query_rows, request_kv, mask_row = packed
        return request_context(request_query_rows, request_kv, mask_row, prefix_kv, valid_tokens)

    outputs = lax.map(one_request, (queries, jnp.moveaxis(fresh_key_value, 1, 0), block_mask))
    return outputs.reshape(REQUEST_COUNT * NEW_TOKENS, QUERY_HEADS * HEAD_WIDTH)
```

```python
import functools
import math

import jax
import jax.numpy as jnp
from jax import lax
from jax.experimental import pallas as pl
from jax.experimental.pallas import tpu as pltpu
from jax.sharding import PartitionSpec as P

PATH = 6
MASKED = -1e30


def attend(chosen, limits, q_ref, fk_ref, fv_ref, *rest):
    k_refs, v_refs, out_ref = rest[:PATH], rest[PATH : 2 * PATH], rest[2 * PATH]
    r = pl.program_id(0)
    tokens, width = q_ref.shape[1], fk_ref.shape[-1]
    slots = k_refs[0].shape[-2]
    group = q_ref.shape[2] // width
    scale = math.log2(math.e) / math.sqrt(width)

    row = lax.broadcasted_iota(jnp.int32, (slots, width), 0)
    marks = [jnp.where(row < limits[r, j], 0.0, MASKED).astype(jnp.bfloat16) for j in range(PATH)]
    keys = jnp.concatenate([k[0, 0, 0] for k in k_refs] + [fk_ref[0, 0]], axis=0)
    marks = jnp.concatenate(marks + [jnp.zeros((tokens, width), jnp.bfloat16)], axis=0)
    keys = jnp.concatenate([keys, marks], axis=1)
    values = jnp.concatenate([v[0, 0, 0] for v in v_refs] + [fv_ref[0, 0]], axis=0)
    values = jnp.concatenate([values, jnp.ones_like(values)], axis=1)
    first = (lax.broadcasted_iota(jnp.int32, (tokens, width), 1) == 0).astype(jnp.bfloat16)
    later = lax.broadcasted_iota(jnp.int32, (tokens, tokens), 0) < lax.broadcasted_iota(
        jnp.int32, (tokens, tokens), 1
    )
    past = PATH * slots
    for g in range(group):
        cols = slice(g * width, (g + 1) * width)
        q = jnp.concatenate([q_ref[0, :, cols], first], axis=1)
        scores = lax.dot_general(
            q, keys, (((1,), (1,)), ((), ())), preferred_element_type=jnp.float32
        )
        own = jnp.where(later, MASKED, scores[:, past:])
        scores = jnp.concatenate([scores[:, :past], own], axis=1)
        peak = jnp.max(scores, axis=1, keepdims=True)
        weights = jnp.exp2((scores - peak) * scale).astype(jnp.bfloat16)
        both = jnp.dot(weights, values, preferred_element_type=jnp.float32)
        out_ref[0, :, cols] = (both[:, :width] / both[:, width:]).astype(jnp.bfloat16)


def attention(queries, fresh, prefix, chosen, limits):
    requests, tokens, heads_wide = queries.shape
    local_kv, slots, width = prefix.shape[2:]
    wide = heads_wide // local_kv

    def block_map(kv, j):
        return lambda r, k, chosen, limits: (kv, chosen[r, j], k, 0, 0)

    def fresh_map(kv):
        return lambda r, k, chosen, limits: (kv, r, 0, k)

    q_spec = pl.BlockSpec((1, tokens, wide), lambda r, k, chosen, limits: (r, 0, k))
    return pl.pallas_call(
        attend,
        out_shape=jax.ShapeDtypeStruct(queries.shape, jnp.bfloat16),
        grid_spec=pltpu.PrefetchScalarGridSpec(
            num_scalar_prefetch=2,
            grid=(requests, local_kv),
            in_specs=[q_spec]
            + [pl.BlockSpec((1, 1, tokens, width), fresh_map(kv)) for kv in (0, 1)]
            + [
                pl.BlockSpec((1, 1, 1, slots, width), block_map(kv, j))
                for kv in (0, 1)
                for j in range(PATH)
            ],
            out_specs=q_spec,
        ),
        compiler_params=pltpu.CompilerParams(vmem_limit_bytes=48 << 20),
    )(chosen, limits, queries, fresh, fresh, *([prefix] * (2 * PATH)))


def per_device(queries, fresh_key_value, prefix_kv, block_mask, valid_tokens):
    requests, length, local_heads, head_size = queries.shape
    blocks = block_mask.shape[1]
    gathered = lax.all_gather(prefix_kv, "req", axis=1, tiled=True)
    order = blocks - jnp.arange(blocks, dtype=jnp.int32)
    ranking = jnp.where(block_mask == 1, order, 0)
    chosen, limits = [], []
    for _ in range(PATH):
        best = jnp.max(ranking, axis=1)
        at = jnp.where(best > 0, blocks - best, 0)
        hit = jnp.arange(blocks)[None, :] == at[:, None]
        chosen.append(at)
        limits.append(jnp.where(best > 0, jnp.sum(jnp.where(hit, valid_tokens[None, :], 0), axis=1), 0))
        ranking = jnp.where(hit, 0, ranking)
    chosen = jnp.stack(chosen, axis=1).astype(jnp.int32)
    limits = jnp.stack(limits, axis=1).astype(jnp.int32)
    q = queries.reshape(requests, length, local_heads * head_size)
    fresh = fresh_key_value.reshape(2, requests, length, -1)
    context = attention(q, fresh, gathered, chosen, limits)
    parts = lax.axis_size("head")
    context = context.reshape(parts, requests * length // parts, local_heads * head_size)
    swapped = lax.all_to_all(context, "head", split_axis=0, concat_axis=0)
    return jnp.concatenate([swapped[i] for i in range(parts)], axis=1)


def solution(mesh):
    return jax.shard_map(
        per_device,
        mesh=mesh,
        in_specs=(
            P("req", None, "head", None),
            P(None, "req", None, "head", None),
            P(None, "req", "head", None, None),
            P("req", None),
            P(),
        ),
        out_specs=P(("req", "head"), None),
        check_vma=False,
    )
```

```python
import functools
import math

import jax
import jax.numpy as jnp
from jax import lax
from jax.experimental import pallas as pl
from jax.experimental.pallas import tpu as pltpu
from jax.sharding import PartitionSpec as P

PATH = 6
MASKED = -1e30


def attend(chosen, limits, q_ref, fk_ref, fv_ref, *rest):
    k_refs, v_refs, out_ref = rest[:PATH], rest[PATH : 2 * PATH], rest[2 * PATH]
    r = pl.program_id(0)
    tokens, width = q_ref.shape[1], fk_ref.shape[-1]
    slots = k_refs[0].shape[-2]
    group = q_ref.shape[2] // width
    scale = math.log2(math.e) / math.sqrt(width)

    row = lax.broadcasted_iota(jnp.int32, (slots, width), 0)
    marks = [jnp.where(row < limits[r, j], 0.0, MASKED).astype(jnp.bfloat16) for j in range(PATH)]
    keys = jnp.concatenate([k[0, 0, 0] for k in k_refs] + [fk_ref[0, 0]], axis=0)
    marks = jnp.concatenate(marks + [jnp.zeros((tokens, width), jnp.bfloat16)], axis=0)
    keys = jnp.concatenate([keys, marks], axis=1)
    values = jnp.concatenate([v[0, 0, 0] for v in v_refs] + [fv_ref[0, 0]], axis=0)
    values = jnp.concatenate([values, jnp.ones_like(values)], axis=1)
    first = (lax.broadcasted_iota(jnp.int32, (tokens, width), 1) == 0).astype(jnp.bfloat16)
    later = lax.broadcasted_iota(jnp.int32, (tokens, tokens), 0) < lax.broadcasted_iota(
        jnp.int32, (tokens, tokens), 1
    )
    past = PATH * slots
    for g in range(group):
        cols = slice(g * width, (g + 1) * width)
        q = jnp.concatenate([q_ref[0, :, cols], first], axis=1)
        scores = lax.dot_general(
            q, keys, (((1,), (1,)), ((), ())), preferred_element_type=jnp.float32
        )
        own = jnp.where(later, MASKED, scores[:, past:])
        scores = jnp.concatenate([scores[:, :past], own], axis=1)
        peak = jnp.max(scores, axis=1, keepdims=True)
        weights = jnp.exp2((scores - peak) * scale).astype(jnp.bfloat16)
        both = jnp.dot(weights, values, preferred_element_type=jnp.float32)
        out_ref[0, :, cols] = (both[:, :width] / both[:, width:]).astype(jnp.bfloat16)


def attention(queries, fresh, prefix, chosen, limits):
    requests, tokens, heads_wide = queries.shape
    local_kv, slots, width = prefix.shape[2:]
    wide = heads_wide // local_kv

    def block_map(kv, j):
        return lambda r, k, chosen, limits: (kv, chosen[r, j], k, 0, 0)

    def fresh_map(kv):
        return lambda r, k, chosen, limits: (kv, r, 0, k)

    q_spec = pl.BlockSpec((1, tokens, wide), lambda r, k, chosen, limits: (r, 0, k))
    return pl.pallas_call(
        attend,
        out_shape=jax.ShapeDtypeStruct(queries.shape, jnp.bfloat16),
        grid_spec=pltpu.PrefetchScalarGridSpec(
            num_scalar_prefetch=2,
            grid=(requests, local_kv),
            in_specs=[q_spec]
            + [pl.BlockSpec((1, 1, tokens, width), fresh_map(kv)) for kv in (0, 1)]
            + [
                pl.BlockSpec((1, 1, 1, slots, width), block_map(kv, j))
                for kv in (0, 1)
                for j in range(PATH)
            ],
            out_specs=q_spec,
        ),
        compiler_params=pltpu.CompilerParams(vmem_limit_bytes=48 << 20),
    )(chosen, limits, queries, fresh, fresh, *([prefix] * (2 * PATH)))


def per_device(queries, fresh_key_value, prefix_kv, block_mask, valid_tokens):
    requests, length, local_heads, head_size = queries.shape
    blocks = block_mask.shape[1]
    order = blocks - jnp.arange(blocks, dtype=jnp.int32)
    ranking = jnp.where(block_mask == 1, order, 0)
    chosen, limits = [], []
    for _ in range(PATH):
        best = jnp.max(ranking, axis=1)
        at = jnp.where(best > 0, blocks - best, 0)
        hit = jnp.arange(blocks)[None, :] == at[:, None]
        chosen.append(at)
        limits.append(jnp.where(best > 0, jnp.sum(jnp.where(hit, valid_tokens[None, :], 0), axis=1), 0))
        ranking = jnp.where(hit, 0, ranking)
    chosen = jnp.stack(chosen, axis=1).astype(jnp.int32)
    limits = jnp.stack(limits, axis=1).astype(jnp.int32)
    local_kv = fresh_key_value.shape[3]
    group = local_heads // local_kv
    parts = lax.axis_size("head")
    rows = requests * length // parts
    gathered = [
        lax.all_gather(prefix_kv[:, :, k : k + 1], "req", axis=1, tiled=True)
        for k in range(local_kv)
    ]
    pieces = []
    for k in range(local_kv):
        q = queries[:, :, k * group : (k + 1) * group].reshape(requests, length, group * head_size)
        fresh = fresh_key_value[:, :, :, k]
        context = attention(q, fresh, gathered[k], chosen, limits)
        context = context.reshape(parts, rows, group * head_size)
        pieces.append(lax.all_to_all(context, "head", split_axis=0, concat_axis=0))
    return jnp.concatenate([piece[i] for i in range(parts) for piece in pieces], axis=1)


def solution(mesh):
    return jax.shard_map(
        per_device,
        mesh=mesh,
        in_specs=(
            P("req", None, "head", None),
            P(None, "req", None, "head", None),
            P(None, "req", "head", None, None),
            P("req", None),
            P(),
        ),
        out_specs=P(("req", "head"), None),
        check_vma=False,
    )
```

```python
import functools
import math

import jax
import jax.numpy as jnp
from jax import lax
from jax.experimental import pallas as pl
from jax.experimental.pallas import tpu as pltpu
from jax.sharding import PartitionSpec as P

PATH = 6
MASKED = -1e30
MESH = pl.DeviceIdType.MESH


def attend(chosen, limits, q_ref, fk_ref, fv_ref, *rest):
    k_refs, v_refs, out_ref = rest[:PATH], rest[PATH : 2 * PATH], rest[2 * PATH]
    r = pl.program_id(0)
    tokens, width = q_ref.shape[1], fk_ref.shape[-1]
    slots = k_refs[0].shape[-2]
    group = q_ref.shape[2] // width
    scale = math.log2(math.e) / math.sqrt(width)

    row = lax.broadcasted_iota(jnp.int32, (slots, width), 0)
    marks = [jnp.where(row < limits[r, j], 0.0, MASKED).astype(jnp.bfloat16) for j in range(PATH)]
    keys = jnp.concatenate([k[0, 0, 0, 0] for k in k_refs] + [fk_ref[0, 0]], axis=0)
    marks = jnp.concatenate(marks + [jnp.zeros((tokens, width), jnp.bfloat16)], axis=0)
    keys = jnp.concatenate([keys, marks], axis=1)
    values = jnp.concatenate([v[0, 0, 0, 0] for v in v_refs] + [fv_ref[0, 0]], axis=0)
    values = jnp.concatenate([values, jnp.ones_like(values)], axis=1)
    first = (lax.broadcasted_iota(jnp.int32, (tokens, width), 1) == 0).astype(jnp.bfloat16)
    later = lax.broadcasted_iota(jnp.int32, (tokens, tokens), 0) < lax.broadcasted_iota(
        jnp.int32, (tokens, tokens), 1
    )
    past = PATH * slots
    for g in range(group):
        cols = slice(g * width, (g + 1) * width)
        q = jnp.concatenate([q_ref[0, :, cols], first], axis=1)
        scores = lax.dot_general(
            q, keys, (((1,), (1,)), ((), ())), preferred_element_type=jnp.float32
        )
        own = jnp.where(later, MASKED, scores[:, past:])
        scores = jnp.concatenate([scores[:, :past], own], axis=1)
        peak = jnp.max(scores, axis=1, keepdims=True)
        weights = jnp.exp2((scores - peak) * scale).astype(jnp.bfloat16)
        both = jnp.dot(weights, values, preferred_element_type=jnp.float32)
        out_ref[0, :, cols] = (both[:, :width] / both[:, width:]).astype(jnp.bfloat16)


def gather_kernel(columns, src, out, up_sem, down_sem, x_sem, near_sem, far_sem, recv_sem, own_sem):
    me = lax.axis_index("req")
    core, x, z = me % 2, (me // 2) % 2, me // 4
    last = columns - 1

    def at(z_at, x_at, core_at):
        return z_at * 4 + x_at * 2 + core_at

    barrier = pltpu.get_barrier_semaphore()

    def greet(device):
        pl.semaphore_signal(barrier, inc=1, device_id={"req": device}, device_id_type=MESH)

    greet(at(z, x, 1 - core))
    greet(at(z, 1 - x, core))

    @pl.when(z > 0)
    def _():
        greet(me - 4)

    @pl.when(z < last)
    def _():
        greet(me + 4)

    peers = 2 + (z > 0).astype(jnp.int32) + (z < last).astype(jnp.int32)
    pl.semaphore_wait(barrier, peers)

    def copy(shard, send_sem, device, from_src=False):
        return pltpu.make_async_remote_copy(
            src_ref=src if from_src else out.at[shard],
            dst_ref=out.at[shard],
            send_sem=send_sem,
            recv_sem=recv_sem.at[shard],
            device_id={"req": device},
            device_id_type=MESH,
        )

    def arrived(shard):
        copy(shard, x_sem.at[0], at(z, 1 - x, core)).wait_recv()

    def always(action):
        action()

    column = [(0, z, None, True)]
    for d in range(1, columns):
        column.append((d, z - d, z >= d, False))
        column.append((columns - 1 + d, z + d, z + d <= last, False))

    def when(condition):
        return always if condition is None else pl.when(condition)

    def z_sends(slot, z_at, from_src):
        shard = at(z_at, x, core)
        found = []
        if slot < columns:
            found.append((z < last, copy(shard, up_sem.at[slot], me + 4, from_src)))
        if slot == 0 or slot >= columns:
            found.append((z > 0, copy(shard, down_sem.at[slot], me - 4, from_src)))
        return found

    def spread(slot, z_at, from_src):
        shard = at(z_at, x, core)
        return [
            copy(shard, x_sem.at[slot], at(z, 1 - x, core), from_src),
            copy(shard, near_sem.at[slot], at(z, x, 1 - core), from_src),
        ]

    def relay(slot, z_at):
        shard = at(z_at, 1 - x, core)
        return shard, copy(shard, far_sem.at[slot], at(z, x, 1 - core))

    def step_column(entry):
        slot, z_at, condition, own = entry

        @when(condition)
        def _():
            if not own:
                arrived(at(z_at, x, core))
            for also, send in z_sends(slot, z_at, own):
                pl.when(also)(send.start)
            for send in spread(slot, z_at, own):
                send.start()

    def step_far(entry):
        slot, z_at, condition, _ = entry

        @when(condition)
        def _():
            shard, send = relay(slot, z_at)
            arrived(shard)
            send.start()

    keep = pltpu.make_async_copy(src, out.at[me], own_sem)
    step_column(column[0])
    keep.start()
    for d in range(1, columns):
        for entry in column[2 * d - 1 : 2 * d + 1]:
            step_column(entry)
        for entry in column[max(2 * d - 3, 0) : 2 * d - 1]:
            step_far(entry)
    for entry in column[-2:]:
        step_far(entry)

    for slot, z_at, condition, own in column:

        @when(condition)
        def _(slot=slot, z_at=z_at, own=own):
            arrived(at(z_at, x, 1 - core))
            arrived(at(z_at, 1 - x, 1 - core))
            for also, send in z_sends(slot, z_at, own):
                pl.when(also)(send.wait_send)
            for send in spread(slot, z_at, own):
                send.wait_send()
            relay(slot, z_at)[1].wait_send()

    keep.wait()


def gather(prefix):
    devices = lax.axis_size("req")
    columns = devices // 4
    slots = 2 * columns - 1
    dma = pltpu.SemaphoreType.DMA
    return pl.pallas_call(
        functools.partial(gather_kernel, columns),
        out_shape=jax.ShapeDtypeStruct((devices,) + prefix.shape, prefix.dtype),
        in_specs=[pl.BlockSpec(memory_space=pl.ANY)],
        out_specs=pl.BlockSpec(memory_space=pl.ANY),
        scratch_shapes=[dma((slots,))] * 5 + [dma((devices,)), dma],
        compiler_params=pltpu.CompilerParams(collective_id=1, has_side_effects=True),
    )(prefix)


def attention(queries, fresh, prefix, chosen, limits, head):
    requests, tokens, wide = queries.shape
    blocks_dev = prefix.shape[2]
    slots, width = prefix.shape[-2:]

    def block_map(kv, j):
        def place(r, chosen, limits):
            return (chosen[r, j] // blocks_dev, kv, chosen[r, j] % blocks_dev, head, 0, 0)

        return place

    def fresh_map(kv):
        return lambda r, chosen, limits: (kv, r, 0, 0)

    q_spec = pl.BlockSpec((1, tokens, wide), lambda r, chosen, limits: (r, 0, 0))
    return pl.pallas_call(
        attend,
        out_shape=jax.ShapeDtypeStruct(queries.shape, jnp.bfloat16),
        grid_spec=pltpu.PrefetchScalarGridSpec(
            num_scalar_prefetch=2,
            grid=(requests,),
            in_specs=[q_spec]
            + [pl.BlockSpec((1, 1, tokens, width), fresh_map(kv)) for kv in (0, 1)]
            + [
                pl.BlockSpec((1, 1, 1, 1, slots, width), block_map(kv, j))
                for kv in (0, 1)
                for j in range(PATH)
            ],
            out_specs=q_spec,
        ),
        compiler_params=pltpu.CompilerParams(vmem_limit_bytes=48 << 20),
    )(chosen, limits, queries, fresh, fresh, *([prefix] * (2 * PATH)))


def per_device(queries, fresh_key_value, prefix_kv, block_mask, valid_tokens):
    requests, length, local_heads, head_size = queries.shape
    blocks = block_mask.shape[1]
    order = blocks - jnp.arange(blocks, dtype=jnp.int32)
    ranking = jnp.where(block_mask == 1, order, 0)
    chosen, limits = [], []
    for _ in range(PATH):
        best = jnp.max(ranking, axis=1)
        at = jnp.where(best > 0, blocks - best, 0)
        hit = jnp.arange(blocks)[None, :] == at[:, None]
        chosen.append(at)
        limits.append(jnp.where(best > 0, jnp.sum(jnp.where(hit, valid_tokens[None, :], 0), axis=1), 0))
        ranking = jnp.where(hit, 0, ranking)
    chosen = jnp.stack(chosen, axis=1).astype(jnp.int32)
    limits = jnp.stack(limits, axis=1).astype(jnp.int32)
    local_kv = fresh_key_value.shape[3]
    group = local_heads // local_kv
    parts = lax.axis_size("head")
    rows = requests * length // parts
    gathered = gather(prefix_kv)
    pieces = []
    for k in range(local_kv):
        q = queries[:, :, k * group : (k + 1) * group].reshape(requests, length, group * head_size)
        fresh = fresh_key_value[:, :, :, k]
        context = attention(q, fresh, gathered, chosen, limits, k)
        context = context.reshape(parts, rows, group * head_size)
        pieces.append(lax.all_to_all(context, "head", split_axis=0, concat_axis=0))
    return jnp.concatenate([piece[i] for i in range(parts) for piece in pieces], axis=1)


def solution(mesh):
    return jax.shard_map(
        per_device,
        mesh=mesh,
        in_specs=(
            P("req", None, "head", None),
            P(None, "req", None, "head", None),
            P(None, "req", "head", None, None),
            P("req", None),
            P(),
        ),
        out_specs=P(("req", "head"), None),
        check_vma=False,
    )
```

```python
import functools
import math

import jax
import jax.numpy as jnp
from jax import lax
from jax.experimental import pallas as pl
from jax.experimental.pallas import tpu as pltpu
from jax.sharding import PartitionSpec as P

PATH = 6
MASKED = -1e30
MESH = pl.DeviceIdType.MESH


def attend(chosen, limits, where, q_ref, fk_ref, fv_ref, *rest):
    k_refs, v_refs, out_ref = rest[:PATH], rest[PATH : 2 * PATH], rest[2 * PATH]
    tokens, width = q_ref.shape[0], fk_ref.shape[-1]
    slots = k_refs[0].shape[-2]
    group = q_ref.shape[1] // width
    scale = math.log2(math.e) / math.sqrt(width)

    row = lax.broadcasted_iota(jnp.int32, (slots, width), 0)
    marks = [jnp.where(row < limits[j], 0.0, MASKED).astype(jnp.bfloat16) for j in range(PATH)]
    keys = jnp.concatenate([k[0, 0, 0, 0] for k in k_refs] + [fk_ref[0, 0]], axis=0)
    marks = jnp.concatenate(marks + [jnp.zeros((tokens, width), jnp.bfloat16)], axis=0)
    keys = jnp.concatenate([keys, marks], axis=1)
    values = jnp.concatenate([v[0, 0, 0, 0] for v in v_refs] + [fv_ref[0, 0]], axis=0)
    values = jnp.concatenate([values, jnp.ones_like(values)], axis=1)
    first = (lax.broadcasted_iota(jnp.int32, (tokens, width), 1) == 0).astype(jnp.bfloat16)
    later = lax.broadcasted_iota(jnp.int32, (tokens, tokens), 0) < lax.broadcasted_iota(
        jnp.int32, (tokens, tokens), 1
    )
    past = PATH * slots
    for g in range(group):
        cols = slice(g * width, (g + 1) * width)
        q = jnp.concatenate([q_ref[:, cols], first], axis=1)
        scores = lax.dot_general(
            q, keys, (((1,), (1,)), ((), ())), preferred_element_type=jnp.float32
        )
        own = jnp.where(later, MASKED, scores[:, past:])
        scores = jnp.concatenate([scores[:, :past], own], axis=1)
        peak = jnp.max(scores, axis=1, keepdims=True)
        weights = jnp.exp2((scores - peak) * scale).astype(jnp.bfloat16)
        both = jnp.dot(weights, values, preferred_element_type=jnp.float32)
        out_ref[:, cols] = (both[:, :width] / both[:, width:]).astype(jnp.bfloat16)


def gather_kernel(columns, src, out, up_sem, down_sem, x_sem, near_sem, far_sem, recv_sem, own_sem):
    me = lax.axis_index("req")
    core, x, z = me % 2, (me // 2) % 2, me // 4
    last = columns - 1

    def at(z_at, x_at, core_at):
        return z_at * 4 + x_at * 2 + core_at

    barrier = pltpu.get_barrier_semaphore()

    def greet(device):
        pl.semaphore_signal(barrier, inc=1, device_id={"req": device}, device_id_type=MESH)

    greet(at(z, x, 1 - core))
    greet(at(z, 1 - x, core))

    @pl.when(z > 0)
    def _():
        greet(me - 4)

    @pl.when(z < last)
    def _():
        greet(me + 4)

    peers = 2 + (z > 0).astype(jnp.int32) + (z < last).astype(jnp.int32)
    pl.semaphore_wait(barrier, peers)

    def copy(shard, send_sem, device, from_src=False):
        return pltpu.make_async_remote_copy(
            src_ref=src if from_src else out.at[shard],
            dst_ref=out.at[shard],
            send_sem=send_sem,
            recv_sem=recv_sem.at[shard],
            device_id={"req": device},
            device_id_type=MESH,
        )

    def arrived(shard):
        copy(shard, x_sem.at[0], at(z, 1 - x, core)).wait_recv()

    def always(action):
        action()

    column = [(0, z, None, True)]
    for d in range(1, columns):
        column.append((d, z - d, z >= d, False))
        column.append((columns - 1 + d, z + d, z + d <= last, False))

    def when(condition):
        return always if condition is None else pl.when(condition)

    def z_sends(slot, z_at, from_src):
        shard = at(z_at, x, core)
        found = []
        if slot < columns:
            found.append((z < last, copy(shard, up_sem.at[slot], me + 4, from_src)))
        if slot == 0 or slot >= columns:
            found.append((z > 0, copy(shard, down_sem.at[slot], me - 4, from_src)))
        return found

    def spread(slot, z_at, from_src):
        shard = at(z_at, x, core)
        return [
            copy(shard, x_sem.at[slot], at(z, 1 - x, core), from_src),
            copy(shard, near_sem.at[slot], at(z, x, 1 - core), from_src),
        ]

    def relay(slot, z_at):
        shard = at(z_at, 1 - x, core)
        return shard, copy(shard, far_sem.at[slot], at(z, x, 1 - core))

    def step_column(entry):
        slot, z_at, condition, own = entry

        @when(condition)
        def _():
            if not own:
                arrived(at(z_at, x, core))
            for also, send in z_sends(slot, z_at, own):
                pl.when(also)(send.start)
            for send in spread(slot, z_at, own):
                send.start()

    def step_far(entry):
        slot, z_at, condition, _ = entry

        @when(condition)
        def _():
            shard, send = relay(slot, z_at)
            arrived(shard)
            send.start()

    keep = pltpu.make_async_copy(src, out.at[me], own_sem)
    step_column(column[0])
    keep.start()
    for d in range(1, columns):
        for entry in column[2 * d - 1 : 2 * d + 1]:
            step_column(entry)
        for entry in column[max(2 * d - 3, 0) : 2 * d - 1]:
            step_far(entry)
    for entry in column[-2:]:
        step_far(entry)

    for slot, z_at, condition, own in column:

        @when(condition)
        def _(slot=slot, z_at=z_at, own=own):
            arrived(at(z_at, x, 1 - core))
            arrived(at(z_at, 1 - x, 1 - core))
            for also, send in z_sends(slot, z_at, own):
                pl.when(also)(send.wait_send)
            for send in spread(slot, z_at, own):
                send.wait_send()
            relay(slot, z_at)[1].wait_send()

    keep.wait()


def gather(prefix):
    devices = lax.axis_size("req")
    columns = devices // 4
    slots = 2 * columns - 1
    dma = pltpu.SemaphoreType.DMA
    return pl.pallas_call(
        functools.partial(gather_kernel, columns),
        out_shape=jax.ShapeDtypeStruct((devices,) + prefix.shape, prefix.dtype),
        in_specs=[pl.BlockSpec(memory_space=pl.ANY)],
        out_specs=pl.BlockSpec(memory_space=pl.ANY),
        scratch_shapes=[dma((slots,))] * 5 + [dma((devices,)), dma],
        compiler_params=pltpu.CompilerParams(collective_id=1, has_side_effects=True),
    )(prefix)


def attention(queries, fresh, prefix, chosen, limits, where, first, count, out_heads):
    tokens = queries.shape[0]
    blocks_dev, local_kv, slots, width = prefix.shape[2:]
    wide = queries.shape[1] // local_kv

    def block_map(kv, j):
        def place(k, chosen, limits, where):
            block = chosen[j]
            return (block // blocks_dev, kv, block % blocks_dev, first + k, 0, 0)

        return place

    def fresh_map(kv):
        return lambda k, chosen, limits, where: (kv, where[0], 0, first + k)

    keys = PATH * slots + tokens
    return pl.pallas_call(
        attend,
        out_shape=jax.ShapeDtypeStruct((tokens, out_heads * wide), jnp.bfloat16),
        grid_spec=pltpu.PrefetchScalarGridSpec(
            num_scalar_prefetch=3,
            grid=(count,),
            in_specs=[pl.BlockSpec((tokens, wide), lambda k, chosen, limits, where: (0, first + k))]
            + [pl.BlockSpec((1, 1, tokens, width), fresh_map(kv)) for kv in (0, 1)]
            + [
                pl.BlockSpec((1, 1, 1, 1, slots, width), block_map(kv, j))
                for kv in (0, 1)
                for j in range(PATH)
            ],
            out_specs=pl.BlockSpec((tokens, wide), lambda k, chosen, limits, where: (0, where[1] + k)),
        ),
        cost_estimate=pl.CostEstimate(
            flops=8 * count * tokens * wide * keys,
            bytes_accessed=count * 4 * (tokens * wide + keys * width),
            transcendentals=count * tokens * wide // width * keys,
        ),
        compiler_params=pltpu.CompilerParams(vmem_limit_bytes=48 << 20),
    )(chosen, limits, where, queries, fresh, fresh, *([prefix] * (2 * PATH)))


def place_kernel(where, piece_ref, whole_ref, out_ref):
    out_ref[...] = piece_ref[...]


def place(whole, piece, where, wide):
    tokens, columns = piece.shape
    return pl.pallas_call(
        place_kernel,
        out_shape=jax.ShapeDtypeStruct(whole.shape, whole.dtype),
        grid_spec=pltpu.PrefetchScalarGridSpec(
            num_scalar_prefetch=1,
            grid=(columns // wide,),
            in_specs=[
                pl.BlockSpec((tokens, wide), lambda k, where: (0, k)),
                pl.BlockSpec(memory_space=pl.ANY),
            ],
            out_specs=pl.BlockSpec((tokens, wide), lambda k, where: (0, where[0] + k)),
        ),
        input_output_aliases={2: 0},
    )(where, piece, whole)


def per_device(queries, fresh_key_value, prefix_kv, block_mask, valid_tokens):
    requests, length, local_heads, head_size = queries.shape
    blocks = block_mask.shape[1]
    order = blocks - jnp.arange(blocks, dtype=jnp.int32)
    ranking = jnp.where(block_mask == 1, order, 0)
    chosen, limits = [], []
    for _ in range(PATH):
        best = jnp.max(ranking, axis=1)
        at = jnp.where(best > 0, blocks - best, 0)
        hit = jnp.arange(blocks)[None, :] == at[:, None]
        chosen.append(at)
        limits.append(jnp.where(best > 0, jnp.sum(jnp.where(hit, valid_tokens[None, :], 0), axis=1), 0))
        ranking = jnp.where(hit, 0, ranking)
    chosen = jnp.stack(chosen, axis=1).astype(jnp.int32)
    limits = jnp.stack(limits, axis=1).astype(jnp.int32)
    local_kv = fresh_key_value.shape[3]
    wide = local_heads // local_kv * head_size
    parts = lax.axis_size("head")
    gathered = gather(prefix_kv)
    fresh = fresh_key_value.reshape(2, requests, length, local_kv * head_size)

    def attend_request(query_rows, request, first, count, base, out_heads):
        pick = functools.partial(lax.dynamic_index_in_dim, axis=0, keepdims=False)
        where = jnp.stack([jnp.int32(request), jnp.int32(base)])
        return attention(
            query_rows, fresh, gathered, pick(chosen, request), pick(limits, request), where, first, count, out_heads
        )

    def flat_queries(source, request):
        rows = lax.dynamic_index_in_dim(source, request, axis=0, keepdims=False)
        return rows.reshape(length, local_heads * head_size)

    if parts != 2 or requests != 2:
        context = jnp.concatenate(
            [attend_request(flat_queries(queries, r), r, 0, local_kv, 0, local_kv) for r in range(requests)]
        )
        context = context.reshape(parts, requests * length // parts, local_kv * wide)
        swapped = lax.all_to_all(context, "head", split_axis=0, concat_axis=0)
        return jnp.concatenate([swapped[i] for i in range(parts)], axis=1)

    mine = lax.axis_index("head")
    other = 1 - mine
    theirs = flat_queries(queries, other)
    cuts = sorted({0, min(1, local_kv), min(2, local_kv), local_kv})
    arrived = []
    source = queries
    for start, end in zip(cuts[:-1], cuts[1:]):
        piece = attend_request(theirs, other, start, end - start, 0, end - start)
        if start == 0:
            source, piece = lax.optimization_barrier((source, piece))
        arrived.append((start, lax.ppermute(piece, "head", [(0, 1), (1, 0)])))
    whole = attend_request(
        flat_queries(source, mine), mine, 0, local_kv, mine * local_kv, parts * local_kv
    )
    for start, piece in arrived:
        whole = place(whole, piece, jnp.stack([other * local_kv + start]), wide)
    return whole


def solution(mesh):
    return jax.shard_map(
        per_device,
        mesh=mesh,
        in_specs=(
            P("req", None, "head", None),
            P(None, "req", None, "head", None),
            P(None, "req", "head", None, None),
            P("req", None),
            P(),
        ),
        out_specs=P(("req", "head"), None),
        check_vma=False,
    )
```

```python
import functools
import math

import jax
import jax.numpy as jnp
from jax import lax
from jax.experimental import pallas as pl
from jax.experimental.pallas import tpu as pltpu
from jax.sharding import PartitionSpec as P

PATH = 6
MASKED = -1e30
MESH = pl.DeviceIdType.MESH


def attend(chosen, limits, where, q_ref, fk_ref, fv_ref, *rest):
    k_refs, v_refs, out_ref = rest[:PATH], rest[PATH : 2 * PATH], rest[2 * PATH]
    tokens, width = q_ref.shape[0], fk_ref.shape[-1]
    slots = k_refs[0].shape[-2]
    group = q_ref.shape[1] // width
    scale = math.log2(math.e) / math.sqrt(width)

    row = lax.broadcasted_iota(jnp.int32, (slots, width), 0)
    marks = [jnp.where(row < limits[j], 0.0, MASKED).astype(jnp.bfloat16) for j in range(PATH)]
    keys = jnp.concatenate([k[0, 0, 0, 0] for k in k_refs] + [fk_ref[0, 0]], axis=0)
    marks = jnp.concatenate(marks + [jnp.zeros((tokens, width), jnp.bfloat16)], axis=0)
    keys = jnp.concatenate([keys, marks], axis=1)
    values = jnp.concatenate([v[0, 0, 0, 0] for v in v_refs] + [fv_ref[0, 0]], axis=0)
    values = jnp.concatenate([values, jnp.ones_like(values)], axis=1)
    first = (lax.broadcasted_iota(jnp.int32, (tokens, width), 1) == 0).astype(jnp.bfloat16)
    later = lax.broadcasted_iota(jnp.int32, (tokens, tokens), 0) < lax.broadcasted_iota(
        jnp.int32, (tokens, tokens), 1
    )
    past = PATH * slots
    for g in range(group):
        cols = slice(g * width, (g + 1) * width)
        q = jnp.concatenate([q_ref[:, cols], first], axis=1)
        scores = lax.dot_general(
            q, keys, (((1,), (1,)), ((), ())), preferred_element_type=jnp.float32
        )
        own = jnp.where(later, MASKED, scores[:, past:])
        scores = jnp.concatenate([scores[:, :past], own], axis=1)
        peak = jnp.max(scores, axis=1, keepdims=True)
        weights = jnp.exp2((scores - peak) * scale).astype(jnp.bfloat16)
        both = jnp.dot(weights, values, preferred_element_type=jnp.float32)
        out_ref[:, cols] = (both[:, :width] / both[:, width:]).astype(jnp.bfloat16)


def gather_kernel(columns, low, high, src, out, up_sem, down_sem, x_sem, near_sem, far_sem, recv_sem, own_sem):
    me = lax.axis_index("req")
    core, x, z = me % 2, (me // 2) % 2, me // 4
    last = columns - 1
    own_part = src.at[:, :, low:high]

    def at(z_at, x_at, core_at):
        return z_at * 4 + x_at * 2 + core_at

    barrier = pltpu.get_barrier_semaphore()

    def greet(device):
        pl.semaphore_signal(barrier, inc=1, device_id={"req": device}, device_id_type=MESH)

    greet(at(z, x, 1 - core))
    greet(at(z, 1 - x, core))

    @pl.when(z > 0)
    def _():
        greet(me - 4)

    @pl.when(z < last)
    def _():
        greet(me + 4)

    peers = 2 + (z > 0).astype(jnp.int32) + (z < last).astype(jnp.int32)
    pl.semaphore_wait(barrier, peers)

    def copy(shard, send_sem, device, from_src=False):
        return pltpu.make_async_remote_copy(
            src_ref=own_part if from_src else out.at[shard],
            dst_ref=out.at[shard],
            send_sem=send_sem,
            recv_sem=recv_sem.at[shard],
            device_id={"req": device},
            device_id_type=MESH,
        )

    def arrived(shard):
        copy(shard, x_sem.at[0], at(z, 1 - x, core)).wait_recv()

    def always(action):
        action()

    column = [(0, z, None, True)]
    for d in range(1, columns):
        column.append((d, z - d, z >= d, False))
        column.append((columns - 1 + d, z + d, z + d <= last, False))

    def when(condition):
        return always if condition is None else pl.when(condition)

    def z_sends(slot, z_at, from_src):
        shard = at(z_at, x, core)
        found = []
        if slot < columns:
            found.append((z < last, copy(shard, up_sem.at[slot], me + 4, from_src)))
        if slot == 0 or slot >= columns:
            found.append((z > 0, copy(shard, down_sem.at[slot], me - 4, from_src)))
        return found

    def spread(slot, z_at, from_src):
        shard = at(z_at, x, core)
        return [
            copy(shard, x_sem.at[slot], at(z, 1 - x, core), from_src),
            copy(shard, near_sem.at[slot], at(z, x, 1 - core), from_src),
        ]

    def relay(slot, z_at):
        shard = at(z_at, 1 - x, core)
        return shard, copy(shard, far_sem.at[slot], at(z, x, 1 - core))

    def step_column(entry):
        slot, z_at, condition, own = entry

        @when(condition)
        def _():
            if not own:
                arrived(at(z_at, x, core))
            for also, send in z_sends(slot, z_at, own):
                pl.when(also)(send.start)
            for send in spread(slot, z_at, own):
                send.start()

    def step_far(entry):
        slot, z_at, condition, _ = entry

        @when(condition)
        def _():
            shard, send = relay(slot, z_at)
            arrived(shard)
            send.start()

    keep = pltpu.make_async_copy(own_part, out.at[me], own_sem)
    step_column(column[0])
    keep.start()
    for d in range(1, columns):
        for entry in column[2 * d - 1 : 2 * d + 1]:
            step_column(entry)
        for entry in column[max(2 * d - 3, 0) : 2 * d - 1]:
            step_far(entry)
    for entry in column[-2:]:
        step_far(entry)

    for slot, z_at, condition, own in column:

        @when(condition)
        def _(slot=slot, z_at=z_at, own=own):
            arrived(at(z_at, x, 1 - core))
            arrived(at(z_at, 1 - x, 1 - core))
            for also, send in z_sends(slot, z_at, own):
                pl.when(also)(send.wait_send)
            for send in spread(slot, z_at, own):
                send.wait_send()
            relay(slot, z_at)[1].wait_send()

    keep.wait()


def gather(prefix, low, high, collective):
    devices = lax.axis_size("req")
    columns = devices // 4
    slots = 2 * columns - 1
    dma = pltpu.SemaphoreType.DMA
    return pl.pallas_call(
        functools.partial(gather_kernel, columns, low, high),
        out_shape=jax.ShapeDtypeStruct(
            (devices,) + prefix.shape[:2] + (high - low,) + prefix.shape[3:], prefix.dtype
        ),
        in_specs=[pl.BlockSpec(memory_space=pl.ANY)],
        out_specs=pl.BlockSpec(memory_space=pl.ANY),
        scratch_shapes=[dma((slots,))] * 5 + [dma((devices,)), dma],
        cost_estimate=pl.CostEstimate(
            flops=0, bytes_accessed=16 * devices * prefix.size * (high - low) // prefix.shape[2], transcendentals=0
        ),
        compiler_params=pltpu.CompilerParams(collective_id=collective, has_side_effects=True),
    )(prefix)


def attention(queries, fresh, prefix, chosen, limits, where, first, count, out_heads, low):
    tokens = queries.shape[0]
    blocks_dev, _, slots, width = prefix.shape[2:]
    wide = queries.shape[1] // (fresh.shape[-1] // width)

    def block_map(kv, j):
        def place(k, chosen, limits, where):
            block = chosen[j]
            return (block // blocks_dev, kv, block % blocks_dev, first - low + k, 0, 0)

        return place

    def fresh_map(kv):
        return lambda k, chosen, limits, where: (kv, where[0], 0, first + k)

    keys = PATH * slots + tokens
    return pl.pallas_call(
        attend,
        out_shape=jax.ShapeDtypeStruct((tokens, out_heads * wide), jnp.bfloat16),
        grid_spec=pltpu.PrefetchScalarGridSpec(
            num_scalar_prefetch=3,
            grid=(count,),
            in_specs=[pl.BlockSpec((tokens, wide), lambda k, chosen, limits, where: (0, first + k))]
            + [pl.BlockSpec((1, 1, tokens, width), fresh_map(kv)) for kv in (0, 1)]
            + [
                pl.BlockSpec((1, 1, 1, 1, slots, width), block_map(kv, j))
                for kv in (0, 1)
                for j in range(PATH)
            ],
            out_specs=pl.BlockSpec((tokens, wide), lambda k, chosen, limits, where: (0, where[1] + k)),
        ),
        cost_estimate=pl.CostEstimate(
            flops=8 * count * tokens * wide * keys,
            bytes_accessed=count * 4 * (tokens * wide + keys * width),
            transcendentals=count * tokens * wide // width * keys,
        ),
        compiler_params=pltpu.CompilerParams(vmem_limit_bytes=48 << 20),
    )(chosen, limits, where, queries, fresh, fresh, *([prefix] * (2 * PATH)))


def place_kernel(where, piece_ref, whole_ref, out_ref):
    out_ref[...] = piece_ref[...]


def place(whole, piece, where, wide):
    tokens, columns = piece.shape
    return pl.pallas_call(
        place_kernel,
        out_shape=jax.ShapeDtypeStruct(whole.shape, whole.dtype),
        grid_spec=pltpu.PrefetchScalarGridSpec(
            num_scalar_prefetch=1,
            grid=(columns // wide,),
            in_specs=[
                pl.BlockSpec((tokens, wide), lambda k, where: (0, k)),
                pl.BlockSpec(memory_space=pl.ANY),
            ],
            out_specs=pl.BlockSpec((tokens, wide), lambda k, where: (0, where[0] + k)),
        ),
        input_output_aliases={2: 0},
    )(where, piece, whole)


def per_device(queries, fresh_key_value, prefix_kv, block_mask, valid_tokens):
    requests, length, local_heads, head_size = queries.shape
    blocks = block_mask.shape[1]
    order = blocks - jnp.arange(blocks, dtype=jnp.int32)
    ranking = jnp.where(block_mask == 1, order, 0)
    chosen, limits = [], []
    for _ in range(PATH):
        best = jnp.max(ranking, axis=1)
        at = jnp.where(best > 0, blocks - best, 0)
        hit = jnp.arange(blocks)[None, :] == at[:, None]
        chosen.append(at)
        limits.append(jnp.where(best > 0, jnp.sum(jnp.where(hit, valid_tokens[None, :], 0), axis=1), 0))
        ranking = jnp.where(hit, 0, ranking)
    chosen = jnp.stack(chosen, axis=1).astype(jnp.int32)
    limits = jnp.stack(limits, axis=1).astype(jnp.int32)
    local_kv = fresh_key_value.shape[3]
    wide = local_heads // local_kv * head_size
    parts = lax.axis_size("head")
    fresh = fresh_key_value.reshape(2, requests, length, local_kv * head_size)

    def attend_request(query_rows, gathered, low, request, first, count, base, out_heads):
        pick = functools.partial(lax.dynamic_index_in_dim, axis=0, keepdims=False)
        where = jnp.stack([jnp.int32(request), jnp.int32(base)])
        return attention(
            query_rows, fresh, gathered, pick(chosen, request), pick(limits, request), where, first, count, out_heads, low
        )

    def flat_queries(source, request):
        rows = lax.dynamic_index_in_dim(source, request, axis=0, keepdims=False)
        return rows.reshape(length, local_heads * head_size)

    if parts != 2 or requests != 2:
        gathered = gather(prefix_kv, 0, local_kv, 1)
        context = jnp.concatenate(
            [attend_request(flat_queries(queries, r), gathered, 0, r, 0, local_kv, 0, local_kv) for r in range(requests)]
        )
        context = context.reshape(parts, requests * length // parts, local_kv * wide)
        swapped = lax.all_to_all(context, "head", split_axis=0, concat_axis=0)
        return jnp.concatenate([swapped[i] for i in range(parts)], axis=1)

    mine = lax.axis_index("head")
    other = 1 - mine
    theirs = flat_queries(queries, other)
    half = max(local_kv // 2, 1)
    arrived, held, source, prefix = [], [], queries, prefix_kv
    for low in range(0, local_kv, half):
        high = min(low + half, local_kv)
        gathered = gather(prefix, low, high, 1 + low // half)
        held.append((low, high, gathered))
        step = half if high < local_kv else 1
        for start in range(low, high, step):
            count = min(step, high - start)
            piece = attend_request(theirs, gathered, low, other, start, count, 0, count)
            if high < local_kv:
                prefix, piece = lax.optimization_barrier((prefix, piece))
            source, piece = lax.optimization_barrier((source, piece))
            arrived.append((start, lax.ppermute(piece, "head", [(0, 1), (1, 0)])))
    own_rows = flat_queries(source, mine)
    low, high, gathered = held[0]
    whole = attend_request(
        own_rows, gathered, low, mine, low, high - low, mine * local_kv, parts * local_kv
    )
    for low, high, gathered in held[1:]:
        piece = attend_request(own_rows, gathered, low, mine, low, high - low, 0, high - low)
        whole = place(whole, piece, jnp.stack([mine * local_kv + low]), wide)
    for start, piece in arrived:
        whole = place(whole, piece, jnp.stack([other * local_kv + start]), wide)
    return whole


def solution(mesh):
    return jax.shard_map(
        per_device,
        mesh=mesh,
        in_specs=(
            P("req", None, "head", None),
            P(None, "req", None, "head", None),
            P(None, "req", "head", None, None),
            P("req", None),
            P(),
        ),
        out_specs=P(("req", "head"), None),
        check_vma=False,
    )
```

```python
import functools
import math

import jax
import jax.numpy as jnp
from jax import lax
from jax.experimental import pallas as pl
from jax.experimental.pallas import tpu as pltpu
from jax.sharding import PartitionSpec as P

PATH = 6
MASKED = -1e30
MESH = pl.DeviceIdType.MESH


def attend(chosen, limits, where, q_ref, fk_ref, fv_ref, *rest):
    k_refs, v_refs, out_ref = rest[:PATH], rest[PATH : 2 * PATH], rest[-1]
    tokens, width = q_ref.shape[0], fk_ref.shape[-1]
    slots = k_refs[0].shape[-2]
    group = q_ref.shape[1] // width
    scale = math.log2(math.e) / math.sqrt(width)

    row = lax.broadcasted_iota(jnp.int32, (slots, width), 0)
    marks = [jnp.where(row < limits[j], 0.0, MASKED).astype(jnp.bfloat16) for j in range(PATH)]
    keys = jnp.concatenate([k[0, 0, 0, 0] for k in k_refs] + [fk_ref[0, 0]], axis=0)
    marks = jnp.concatenate(marks + [jnp.zeros((tokens, width), jnp.bfloat16)], axis=0)
    keys = jnp.concatenate([keys, marks], axis=1)
    values = jnp.concatenate([v[0, 0, 0, 0] for v in v_refs] + [fv_ref[0, 0]], axis=0)
    values = jnp.concatenate([values, jnp.ones_like(values)], axis=1)
    first = (lax.broadcasted_iota(jnp.int32, (tokens, width), 1) == 0).astype(jnp.bfloat16)
    later = lax.broadcasted_iota(jnp.int32, (tokens, tokens), 0) < lax.broadcasted_iota(
        jnp.int32, (tokens, tokens), 1
    )
    past = PATH * slots
    for g in range(group):
        cols = slice(g * width, (g + 1) * width)
        q = jnp.concatenate([q_ref[:, cols], first], axis=1)
        scores = lax.dot_general(
            q, keys, (((1,), (1,)), ((), ())), preferred_element_type=jnp.float32
        )
        own = jnp.where(later, MASKED, scores[:, past:])
        scores = jnp.concatenate([scores[:, :past], own], axis=1)
        peak = jnp.max(scores, axis=1, keepdims=True)
        weights = jnp.exp2((scores - peak) * scale).astype(jnp.bfloat16)
        both = jnp.dot(weights, values, preferred_element_type=jnp.float32)
        out_ref[:, cols] = (both[:, :width] / both[:, width:]).astype(jnp.bfloat16)


def gather_kernel(columns, low, high, src, out, up_sem, down_sem, x_sem, near_sem, far_sem, recv_sem, own_sem):
    me = lax.axis_index("req")
    core, x, z = me % 2, (me // 2) % 2, me // 4
    last = columns - 1
    own_part = src.at[:, :, low:high]

    def at(z_at, x_at, core_at):
        return z_at * 4 + x_at * 2 + core_at

    barrier = pltpu.get_barrier_semaphore()

    def greet(device):
        pl.semaphore_signal(barrier, inc=1, device_id={"req": device}, device_id_type=MESH)

    greet(at(z, x, 1 - core))
    greet(at(z, 1 - x, core))

    @pl.when(z > 0)
    def _():
        greet(me - 4)

    @pl.when(z < last)
    def _():
        greet(me + 4)

    peers = 2 + (z > 0).astype(jnp.int32) + (z < last).astype(jnp.int32)
    pl.semaphore_wait(barrier, peers)

    def copy(shard, send_sem, device, from_src=False):
        return pltpu.make_async_remote_copy(
            src_ref=own_part if from_src else out.at[shard],
            dst_ref=out.at[shard],
            send_sem=send_sem,
            recv_sem=recv_sem.at[shard],
            device_id={"req": device},
            device_id_type=MESH,
        )

    def arrived(shard):
        copy(shard, x_sem.at[0], at(z, 1 - x, core)).wait_recv()

    def always(action):
        action()

    column = [(0, z, None, True)]
    for d in range(1, columns):
        column.append((d, z - d, z >= d, False))
        column.append((columns - 1 + d, z + d, z + d <= last, False))

    def when(condition):
        return always if condition is None else pl.when(condition)

    def z_sends(slot, z_at, from_src):
        shard = at(z_at, x, core)
        found = []
        if slot < columns:
            found.append((z < last, copy(shard, up_sem.at[slot], me + 4, from_src)))
        if slot == 0 or slot >= columns:
            found.append((z > 0, copy(shard, down_sem.at[slot], me - 4, from_src)))
        return found

    def spread(slot, z_at, from_src):
        shard = at(z_at, x, core)
        return [
            copy(shard, x_sem.at[slot], at(z, 1 - x, core), from_src),
            copy(shard, near_sem.at[slot], at(z, x, 1 - core), from_src),
        ]

    def relay(slot, z_at):
        shard = at(z_at, 1 - x, core)
        return shard, copy(shard, far_sem.at[slot], at(z, x, 1 - core))

    def step_column(entry):
        slot, z_at, condition, own = entry

        @when(condition)
        def _():
            if not own:
                arrived(at(z_at, x, core))
            for also, send in z_sends(slot, z_at, own):
                pl.when(also)(send.start)
            for send in spread(slot, z_at, own):
                send.start()

    def step_far(entry):
        slot, z_at, condition, _ = entry

        @when(condition)
        def _():
            shard, send = relay(slot, z_at)
            arrived(shard)
            send.start()

    keep = pltpu.make_async_copy(own_part, out.at[me], own_sem)
    step_column(column[0])
    keep.start()
    for d in range(1, columns):
        for entry in column[2 * d - 1 : 2 * d + 1]:
            step_column(entry)
        for entry in column[max(2 * d - 3, 0) : 2 * d - 1]:
            step_far(entry)
    for entry in column[-2:]:
        step_far(entry)

    for slot, z_at, condition, own in column:

        @when(condition)
        def _(slot=slot, z_at=z_at, own=own):
            arrived(at(z_at, x, 1 - core))
            arrived(at(z_at, 1 - x, 1 - core))
            for also, send in z_sends(slot, z_at, own):
                pl.when(also)(send.wait_send)
            for send in spread(slot, z_at, own):
                send.wait_send()
            relay(slot, z_at)[1].wait_send()

    keep.wait()


def gather(prefix, low, high, collective):
    devices = lax.axis_size("req")
    columns = devices // 4
    slots = 2 * columns - 1
    dma = pltpu.SemaphoreType.DMA
    return pl.pallas_call(
        functools.partial(gather_kernel, columns, low, high),
        out_shape=jax.ShapeDtypeStruct(
            (devices,) + prefix.shape[:2] + (high - low,) + prefix.shape[3:], prefix.dtype
        ),
        in_specs=[pl.BlockSpec(memory_space=pl.ANY)],
        out_specs=pl.BlockSpec(memory_space=pl.ANY),
        scratch_shapes=[dma((slots,))] * 5 + [dma((devices,)), dma],
        cost_estimate=pl.CostEstimate(
            flops=0, bytes_accessed=16 * devices * prefix.size * (high - low) // prefix.shape[2], transcendentals=0
        ),
        compiler_params=pltpu.CompilerParams(collective_id=collective, has_side_effects=True),
    )(prefix)


def attention(queries, fresh, prefix, chosen, limits, where, first, count, out_heads, low, into=()):
    tokens = queries.shape[0]
    blocks_dev, _, slots, width = prefix.shape[2:]
    wide = queries.shape[1] // (fresh.shape[-1] // width)

    def block_map(kv, j):
        def place(k, chosen, limits, where):
            block = chosen[j]
            return (block // blocks_dev, kv, block % blocks_dev, first - low + k, 0, 0)

        return place

    def fresh_map(kv):
        return lambda k, chosen, limits, where: (kv, where[0], 0, first + k)

    keys = PATH * slots + tokens
    return pl.pallas_call(
        attend,
        out_shape=jax.ShapeDtypeStruct((tokens, out_heads * wide), jnp.bfloat16),
        grid_spec=pltpu.PrefetchScalarGridSpec(
            num_scalar_prefetch=3,
            grid=(count,),
            in_specs=[pl.BlockSpec((tokens, wide), lambda k, chosen, limits, where: (0, first + k))]
            + [pl.BlockSpec((1, 1, tokens, width), fresh_map(kv)) for kv in (0, 1)]
            + [
                pl.BlockSpec((1, 1, 1, 1, slots, width), block_map(kv, j))
                for kv in (0, 1)
                for j in range(PATH)
            ]
            + [pl.BlockSpec(memory_space=pl.ANY)] * len(into),
            out_specs=pl.BlockSpec((tokens, wide), lambda k, chosen, limits, where: (0, where[1] + k)),
        ),
        input_output_aliases={6 + 2 * PATH: 0} if into else {},
        cost_estimate=pl.CostEstimate(
            flops=8 * count * tokens * wide * keys,
            bytes_accessed=count * 4 * (tokens * wide + keys * width),
            transcendentals=count * tokens * wide // width * keys,
        ),
        compiler_params=pltpu.CompilerParams(vmem_limit_bytes=48 << 20),
    )(chosen, limits, where, queries, fresh, fresh, *([prefix] * (2 * PATH)), *into)


def place_kernel(where, piece_ref, whole_ref, out_ref):
    out_ref[...] = piece_ref[...]


def place(whole, piece, where, wide):
    tokens, columns = piece.shape
    return pl.pallas_call(
        place_kernel,
        out_shape=jax.ShapeDtypeStruct(whole.shape, whole.dtype),
        grid_spec=pltpu.PrefetchScalarGridSpec(
            num_scalar_prefetch=1,
            grid=(columns // wide,),
            in_specs=[
                pl.BlockSpec((tokens, wide), lambda k, where: (0, k)),
                pl.BlockSpec(memory_space=pl.ANY),
            ],
            out_specs=pl.BlockSpec((tokens, wide), lambda k, where: (0, where[0] + k)),
        ),
        input_output_aliases={2: 0},
    )(where, piece, whole)


def per_device(queries, fresh_key_value, prefix_kv, block_mask, valid_tokens):
    requests, length, local_heads, head_size = queries.shape
    blocks = block_mask.shape[1]
    order = blocks - jnp.arange(blocks, dtype=jnp.int32)
    ranking = jnp.where(block_mask == 1, order, 0)
    chosen, limits = [], []
    for _ in range(PATH):
        best = jnp.max(ranking, axis=1)
        at = jnp.where(best > 0, blocks - best, 0)
        hit = jnp.arange(blocks)[None, :] == at[:, None]
        chosen.append(at)
        limits.append(jnp.where(best > 0, jnp.sum(jnp.where(hit, valid_tokens[None, :], 0), axis=1), 0))
        ranking = jnp.where(hit, 0, ranking)
    chosen = jnp.stack(chosen, axis=1).astype(jnp.int32)
    limits = jnp.stack(limits, axis=1).astype(jnp.int32)
    local_kv = fresh_key_value.shape[3]
    wide = local_heads // local_kv * head_size
    parts = lax.axis_size("head")
    fresh = fresh_key_value.reshape(2, requests, length, local_kv * head_size)

    def attend_request(query_rows, gathered, low, request, first, count, base, out_heads, into=()):
        pick = functools.partial(lax.dynamic_index_in_dim, axis=0, keepdims=False)
        where = jnp.stack([jnp.int32(request), jnp.int32(base)])
        return attention(
            query_rows, fresh, gathered, pick(chosen, request), pick(limits, request), where, first, count, out_heads, low, into
        )

    def flat_queries(source, request):
        rows = lax.dynamic_index_in_dim(source, request, axis=0, keepdims=False)
        return rows.reshape(length, local_heads * head_size)

    if parts != 2 or requests != 2:
        gathered = gather(prefix_kv, 0, local_kv, 1)
        context = jnp.concatenate(
            [attend_request(flat_queries(queries, r), gathered, 0, r, 0, local_kv, 0, local_kv) for r in range(requests)]
        )
        context = context.reshape(parts, requests * length // parts, local_kv * wide)
        swapped = lax.all_to_all(context, "head", split_axis=0, concat_axis=0)
        return jnp.concatenate([swapped[i] for i in range(parts)], axis=1)

    mine = lax.axis_index("head")
    other = 1 - mine
    theirs = flat_queries(queries, other)
    half = max(local_kv - 1, 1)
    arrived, held, source, prefix = [], [], queries, prefix_kv
    for low in range(0, local_kv, half):
        high = min(low + half, local_kv)
        gathered = gather(prefix, low, high, 1 + low // half)
        held.append((low, high, gathered))
        step = half if high < local_kv else 1
        for start in range(low, high, step):
            count = min(step, high - start)
            piece = attend_request(theirs, gathered, low, other, start, count, 0, count)
            if high < local_kv:
                prefix, piece = lax.optimization_barrier((prefix, piece))
            source, piece = lax.optimization_barrier((source, piece))
            arrived.append((start, lax.ppermute(piece, "head", [(0, 1), (1, 0)])))
    own_rows = flat_queries(source, mine)
    low, high, gathered = held[0]
    whole = attend_request(
        own_rows, gathered, low, mine, low, high - low, mine * local_kv, parts * local_kv
    )
    for low, high, gathered in held[1:]:
        whole = attend_request(
            own_rows, gathered, low, mine, low, high - low, mine * local_kv + low, parts * local_kv, (whole,)
        )
    for start, piece in arrived:
        whole = place(whole, piece, jnp.stack([other * local_kv + start]), wide)
    return whole


def solution(mesh):
    return jax.shard_map(
        per_device,
        mesh=mesh,
        in_specs=(
            P("req", None, "head", None),
            P(None, "req", None, "head", None),
            P(None, "req", "head", None, None),
            P("req", None),
            P(),
        ),
        out_specs=P(("req", "head"), None),
        check_vma=False,
    )
```
